32 devices in a mesh: grp: 2 (over y), seq: 4 (over z), head: 4 (over x, core).
Axes of the slice: x: 2, y: 2, z: 4, core: 2. Of those that a mesh axis runs over, the one named last changes fastest.
Arguments:
- queries: bfloat16 [3072, 4096], P(('grp', 'seq'), 'head'), parts along dimension 0, may hold values from -6 to 6
- keys: bfloat16 [3072, 2048], P(('grp', 'seq'), 'head'), parts along dimension 0, may hold values from -6 to 6
- values: bfloat16 [3072, 2048], P(('grp', 'seq'), 'head'), parts along dimension 0, may hold values from -16 to 16
- out_weight: bfloat16 [4096, 5376], P('head'), may hold values from -0.5 to 0.5
Outputs:
- mixed: bfloat16 [3072, 5376], P(('grp', 'seq', 'head')), parts along dimension 0
The draws below stay inside these ranges and needn't reach their ends.
There are 2 independent parts, one for each index of `grp`. The reference program is written for one: setup_inputs(seed, part) draws one part's arguments, and reference() takes and returns one part's arrays. A program takes and returns all parts, laid end to end along the dimension named above; an argument that names none is the same for every part. Nothing has to cross between parts.
All inputs are finite; a program needn't handle non-finite values.
Results may differ from the reference program's by a relative error of at most 0.02.
Values may be sent and summed in bfloat16 or wider, within the bound.
A program may use at most 64 MiB of HBM per device.

```python
import jax
import jax.numpy as jnp
from jax import lax

D = 5376
QUERY_HEADS = 32
KEY_VALUE_HEADS = 16
HEAD_SIZE = 128
BLOCK_TOKENS = 384
SEQUENCE_TOKENS = 1536
N_SEQ = 4
N_HEAD = 4


def paired_draw(key):
    base = jax.random.fold_in(key, 11)
    query_seed, key_random_seed = jax.random.split(base, 2)
    query_drawn = jnp.clip(jax.random.normal(query_seed, (SEQUENCE_TOKENS, QUERY_HEADS * HEAD_SIZE), jnp.float32), -4.0, 4.0)
    sampled_keys = jnp.clip(jax.random.normal(key_random_seed, (SEQUENCE_TOKENS, KEY_VALUE_HEADS * HEAD_SIZE), jnp.float32), -4.0, 4.0)
    return (query_drawn, sampled_keys)


def draw_queries(key, part):
    return paired_draw(key)[0].astype(jnp.bfloat16)


def draw_keys(key, part):
    return paired_draw(key)[1].astype(jnp.bfloat16)


def steps_of(stream_key, shape, cuts, smallest, high):
    loudness, own = 1.0, jax.random.fold_in(stream_key, 6)
    for position, blocks in cuts:
        steps = jnp.exp(jax.random.uniform(jax.random.fold_in(own, position), (blocks,), jnp.float32, smallest / len(cuts), high / len(cuts)))
        loudness = loudness * jnp.repeat(steps, shape[position] // blocks).reshape([-1 if axis == position else 1 for axis in range(len(shape))])
    return loudness


def gaussian(rng, dims, deviation, bound, cuts=(), held_as=jnp.bfloat16):
    drawn = deviation * jax.random.normal(rng, dims, jnp.float32)
    if cuts:
        drawn = drawn * steps_of(rng, dims, cuts, -0.22, 0.18)
    return jnp.clip(drawn, -bound, bound).astype(held_as)


def setup_inputs(seed: int = 0, part: int = 0) -> dict:
    seeds = jax.random.split(jax.random.key(seed), 5)
    part_splits = jax.random.split(jax.random.fold_in(seeds[4], part), 5)
    return {
        "queries": draw_queries(jax.random.fold_in(jax.random.fold_in(seeds[4], part), 71), part),
        "keys": draw_keys(jax.random.fold_in(jax.random.fold_in(seeds[4], part), 71), part),
        "values": gaussian(part_splits[2], (SEQUENCE_TOKENS, KEY_VALUE_HEADS * HEAD_SIZE), 4.0, 16.0, ((0, 4), (1, 4))),
        "out_weight": gaussian(seeds[3], (QUERY_HEADS * HEAD_SIZE, D), HEAD_SIZE ** -0.5, 0.5, ((0, 4),)),
    }


attn_scale = 168.0 ** -0.5


def block_attention(block, queries, keys, values):
    distances = [0] + [1 << step_level for step_level in range(N_SEQ.bit_length() - 1)]
    begin = (block * BLOCK_TOKENS).astype(jnp.int32)
    query_row_block = lax.dynamic_slice_in_dim(queries, begin, BLOCK_TOKENS, 0).astype(jnp.float32)
    causal = jnp.arange(BLOCK_TOKENS)[:, None] >= jnp.arange(BLOCK_TOKENS)[None, :]
    key_parts = []
    value_parts = []
    mask_parts = []
    for distance in distances:
        source = (jnp.maximum(block - distance, 0) * BLOCK_TOKENS).astype(jnp.int32)
        key_parts.append(lax.dynamic_slice_in_dim(keys, source, BLOCK_TOKENS, 0))
        value_parts.append(lax.dynamic_slice_in_dim(values, source, BLOCK_TOKENS, 0))
        if distance == 0:
            mask_parts.append(causal)
        else:
            mask_parts.append(jnp.broadcast_to(block >= distance, (BLOCK_TOKENS, BLOCK_TOKENS)))
    full_keys = jnp.concatenate(key_parts, axis=0).astype(jnp.float32)
    full_values = jnp.concatenate(value_parts, axis=0).astype(jnp.float32)
    visible = jnp.concatenate(mask_parts, axis=1)
    group_width = QUERY_HEADS // KEY_VALUE_HEADS
    query_head_stack = query_row_block.reshape(BLOCK_TOKENS, KEY_VALUE_HEADS, group_width, HEAD_SIZE)
    key_head_stack = full_keys.reshape(-1, KEY_VALUE_HEADS, HEAD_SIZE)
    value_head_stack = full_values.reshape(-1, KEY_VALUE_HEADS, HEAD_SIZE)
    scores = jnp.einsum("tkgd,skd->kgts", query_head_stack, key_head_stack) * attn_scale
    masked = jnp.where(visible, scores, -jnp.inf)
    row_max = jnp.max(masked, axis=-1, keepdims=True)
    shifted = jnp.exp(masked - row_max)
    row_sum = jnp.sum(shifted, axis=-1, keepdims=True)
    weights = (shifted / row_sum).astype(jnp.bfloat16).astype(jnp.float32)
    attended = jnp.einsum("kgts,skd->tkgd", weights, value_head_stack)
    return attended.astype(jnp.bfloat16).reshape(BLOCK_TOKENS, QUERY_HEADS * HEAD_SIZE)


def reference(queries, keys, values, out_weight):
    blocks = jnp.arange(N_SEQ, dtype=jnp.int32)
    attended = lax.map(lambda block: block_attention(block, queries, keys, values), blocks)
    attended = attended.reshape(SEQUENCE_TOKENS, QUERY_HEADS * HEAD_SIZE)
    band = QUERY_HEADS * HEAD_SIZE // N_HEAD

    def add_group(carry, group_index):
        start_col = (group_index * band).astype(jnp.int32)
        picked = lax.dynamic_slice_in_dim(attended, start_col, band, 1)
        weight_rows = lax.dynamic_slice_in_dim(out_weight, start_col, band, 0)
        partial_value = jnp.dot(picked, weight_rows, preferred_element_type=jnp.float32)
        partial_value = lax.optimization_barrier(partial_value.astype(jnp.bfloat16)).astype(jnp.float32)
        return carry + partial_value, None

    summed, _ = lax.scan(add_group, jnp.zeros((SEQUENCE_TOKENS, D), jnp.float32), jnp.arange(N_HEAD, dtype=jnp.int32))
    return summed.astype(jnp.bfloat16)
```

```python
import functools
import math

import jax
import jax.numpy as jnp
from jax import lax
from jax.experimental import pallas as pl
from jax.experimental.pallas import tpu as pltpu
from jax.sharding import PartitionSpec as P

QUERY_HEADS = 32
KEY_VALUE_HEADS = 16
HEAD_SIZE = 128
GROUP_WIDTH = QUERY_HEADS // KEY_VALUE_HEADS
CORES = 2

score_scale = 168.0 ** (-0.5) * math.log2(math.e)
MASKED = -1e30

MESH = pl.DeviceIdType.MESH


def layer_kernel(
    n_seq, n_head,
    q_hbm, k_hbm, v_hbm, w_hbm, out_hbm,
    q_buf, kv_buf, top, total, mix, attended, w_buf, partial, core_out, core_in,
    chip_out, chip_in, kept, out_buf,
    q_sem, kv_sem, w_sem, z_send, z_recv, core_send, core_recv, chip_send, chip_recv, out_sem,
):
    kv_local, _, rows, _ = kv_buf.shape[1:]
    n_chunk, _, chunk = w_buf.shape
    block = rows // n_head
    n_chip = n_head // CORES
    reaches = [1 << level for level in range(n_seq.bit_length() - 1)]
    hops = [1] + reaches[:-1] if reaches else []
    seq = lax.axis_index("seq")
    head = lax.axis_index("head")
    chip, core = head // CORES, head % CORES
    core_peer = chip * CORES + 1 - core

    def columns(index, width):
        return pl.ds(pl.multiple_of(index * width, 128), width)

    def kv_load(c, which):
        source = (k_hbm, v_hbm)[which]
        return pltpu.make_async_copy(
            source.at[:, columns(c, HEAD_SIZE)], kv_buf.at[0, c, which], kv_sem.at[c, which]
        )

    def q_load(c, g):
        return pltpu.make_async_copy(
            q_hbm.at[:, columns(c * GROUP_WIDTH + g, HEAD_SIZE)], q_buf.at[c, g], q_sem.at[c, g]
        )

    def w_load(j):
        return pltpu.make_async_copy(w_hbm.at[:, columns(j, chunk)], w_buf.at[j], w_sem.at[j])

    def z_copy(level, c):
        hop = hops[level]
        return pltpu.make_async_remote_copy(
            src_ref=kv_buf.at[level, c],
            dst_ref=kv_buf.at[level + 1, c],
            send_sem=z_send.at[level, c],
            recv_sem=z_recv.at[level, c],
            device_id={"seq": lax.rem(seq + hop, n_seq)},
            device_id_type=MESH,
        )

    def z_sends(level):
        needed = reaches[level - 1] if level else 0
        return jnp.logical_and(seq >= needed, seq + hops[level] < n_seq)

    def core_copy(j):
        return pltpu.make_async_remote_copy(
            src_ref=core_out.at[j],
            dst_ref=core_in.at[j],
            send_sem=core_send.at[j],
            recv_sem=core_recv.at[j],
            device_id={"head": core_peer},
            device_id_type=MESH,
        )

    def chip_copy(j, offset):
        return pltpu.make_async_remote_copy(
            src_ref=chip_out.at[j, offset - 1],
            dst_ref=chip_in.at[j, offset - 1],
            send_sem=chip_send.at[j, offset - 1],
            recv_sem=chip_recv.at[j, offset - 1],
            device_id={"head": lax.rem(chip + offset, n_chip) * CORES + core},
            device_id_type=MESH,
        )

    def out_copy(j):
        return pltpu.make_async_copy(
            out_buf.at[j], out_hbm.at[:, columns(j, chunk)], out_sem.at[j]
        )

    def loop(low, high, body):
        def step(i, carry):
            body(i)
            return carry

        lax.fori_loop(low, high, step, 0)

    barrier = pltpu.get_barrier_semaphore()
    expected = jnp.int32(n_chip)
    for distance in sorted(set(hops)):
        later, earlier = seq + distance < n_seq, seq >= distance

        @pl.when(later)
        def _():
            pl.semaphore_signal(
                barrier, inc=1, device_id={"seq": seq + distance}, device_id_type=MESH
            )

        @pl.when(earlier)
        def _():
            pl.semaphore_signal(
                barrier, inc=1, device_id={"seq": seq - distance}, device_id_type=MESH
            )

        expected += later.astype(jnp.int32) + earlier.astype(jnp.int32)
    pl.semaphore_signal(barrier, inc=1, device_id={"head": core_peer}, device_id_type=MESH)
    for offset in range(1, n_chip):
        pl.semaphore_signal(
            barrier,
            inc=1,
            device_id={"head": lax.rem(chip + offset, n_chip) * CORES + core},
            device_id_type=MESH,
        )

    for c in range(kv_local):
        kv_load(c, 0).start()
        kv_load(c, 1).start()
    for c in range(kv_local):
        for g in range(GROUP_WIDTH):
            q_load(c, g).start()
    pl.semaphore_wait(barrier, expected)

    def send_own(c):
        kv_load(c, 0).wait()
        kv_load(c, 1).wait()
        if reaches:
            @pl.when(z_sends(0))
            def _():
                z_copy(0, c).start()

    loop(0, kv_local, send_own)
    for j in range(n_chunk):
        w_load(j).start()

    def scores_of(level, c):
        stacked = q_buf[c].reshape(GROUP_WIDTH * rows, HEAD_SIZE)
        return score_scale * lax.dot_general(
            stacked, kv_buf[level, c, 0], (((1,), (1,)), ((), ())),
            preferred_element_type=jnp.float32,
        )

    def mixed_values(level, c, shifted):
        return jnp.dot(
            shifted.astype(jnp.bfloat16), kv_buf[level, c, 1], preferred_element_type=jnp.float32
        )

    def own_block(c):
        for g in range(GROUP_WIDTH):
            q_load(c, g).wait()
        shape = (GROUP_WIDTH, rows, rows)
        causal = lax.broadcasted_iota(jnp.int32, shape, 1) >= lax.broadcasted_iota(
            jnp.int32, shape, 2
        )
        scores = scores_of(0, c).reshape(shape)
        scores = jnp.where(causal, scores, MASKED).reshape(GROUP_WIDTH * rows, rows)
        row_max = jnp.max(scores, axis=-1, keepdims=True)
        shifted = jnp.exp2(scores - row_max)
        top[c] = row_max
        total[c] = jnp.sum(shifted, axis=-1, keepdims=True)
        mix[c] = mixed_values(0, c, shifted)

    def earlier_block(level, c):
        scores = scores_of(level, c)
        before = top[c]
        row_max = jnp.maximum(before, jnp.max(scores, axis=-1, keepdims=True))
        fade = jnp.exp2(before - row_max)
        shifted = jnp.exp2(scores - row_max)
        top[c] = row_max
        total[c] = total[c] * fade + jnp.sum(shifted, axis=-1, keepdims=True)
        mix[c] = mix[c] * fade + mixed_values(level, c, shifted)

    def finish(c):
        done = (mix[c] / total[c]).astype(jnp.bfloat16)
        for g in range(GROUP_WIDTH):
            attended[:, columns(c * GROUP_WIDTH + g, HEAD_SIZE)] = done[g * rows : (g + 1) * rows]

    loop(0, kv_local, own_block)
    for level, distance in enumerate(reaches, 1):

        def arrived(c):
            @pl.when(seq >= distance)
            def _():
                z_copy(level - 1, c).wait_recv()
                if level < len(reaches):
                    @pl.when(z_sends(level))
                    def _():
                        z_copy(level, c).start()

                earlier_block(level, c)

            if level == len(reaches):
                finish(c)

        loop(0, kv_local, arrived)
    if not reaches:
        loop(0, kv_local, finish)

    def project(j):
        w_load(j).wait()
        slot = lax.rem(j, 2)
        partial[slot] = jnp.dot(attended[...], w_buf[j], preferred_element_type=jnp.float32)
        for x in range(n_chip):
            start = pl.multiple_of((x * CORES + 1 - core) * block, 8)
            core_out[j, x] = partial[slot, pl.ds(start, block), :].astype(jnp.bfloat16)
        core_copy(j).start()

    def exchange(j):
        slot = lax.rem(j, 2)
        core_copy(j).wait_recv()

        def both_cores(x):
            start = pl.multiple_of((x * CORES + core) * block, 8)
            return partial[slot, pl.ds(start, block), :] + core_in[j, x].astype(jnp.float32)

        for offset in range(1, n_chip):
            chip_out[j, offset - 1] = both_cores(lax.rem(chip + offset, n_chip)).astype(
                jnp.bfloat16
            )
            chip_copy(j, offset).start()
        kept[j] = both_cores(chip)

    def collect(j):
        summed = kept[j]
        for offset in range(1, n_chip):
            chip_copy(j, offset).wait_recv()
            summed += chip_in[j, offset - 1].astype(jnp.float32)
        out_buf[j] = summed.astype(jnp.bfloat16)
        out_copy(j).start()

    project(0)

    def step(j):
        project(j)
        exchange(j - 1)

    loop(1, n_chunk, step)
    exchange(n_chunk - 1)
    loop(0, n_chunk, collect)

    def settle(j):
        core_copy(j).wait_send()
        for offset in range(1, n_chip):
            chip_copy(j, offset).wait_send()
        out_copy(j).wait()

    loop(0, n_chunk, settle)
    for level in range(len(reaches)):

        @pl.when(z_sends(level))
        def _():
            loop(0, kv_local, lambda c: z_copy(level, c).wait_send())


def solution(mesh):
    n_seq, n_head = mesh.shape["seq"], mesh.shape["head"]

    def on_device(queries, keys, values, out_weight):
        rows = queries.shape[0]
        depth, width = out_weight.shape
        kv_local = keys.shape[1] // HEAD_SIZE
        block = rows // n_head
        n_chip = n_head // CORES
        levels = n_seq.bit_length() - 1
        chunk = max(c for c in range(128, 769, 128) if width % c == 0)
        n_chunk = width // chunk
        stacked = GROUP_WIDTH * rows
        bf16, f32, dma = jnp.bfloat16, jnp.float32, pltpu.SemaphoreType.DMA
        anywhere = pl.BlockSpec(memory_space=pl.ANY)
        others = max(1, n_chip - 1)
        return pl.pallas_call(
            functools.partial(layer_kernel, n_seq, n_head),
            out_shape=jax.ShapeDtypeStruct((block, width), bf16),
            in_specs=[anywhere] * 4,
            out_specs=anywhere,
            scratch_shapes=[
                pltpu.VMEM((kv_local, GROUP_WIDTH, rows, HEAD_SIZE), bf16),
                pltpu.VMEM((levels + 1, kv_local, 2, rows, HEAD_SIZE), bf16),
                pltpu.VMEM((kv_local, stacked, 1), f32),
                pltpu.VMEM((kv_local, stacked, 1), f32),
                pltpu.VMEM((kv_local, stacked, HEAD_SIZE), f32),
                pltpu.VMEM((rows, depth), bf16),
                pltpu.VMEM((n_chunk, depth, chunk), bf16),
                pltpu.VMEM((2, rows, chunk), f32),
                pltpu.VMEM((n_chunk, n_chip, block, chunk), bf16),
                pltpu.VMEM((n_chunk, n_chip, block, chunk), bf16),
                pltpu.VMEM((n_chunk, others, block, chunk), bf16),
                pltpu.VMEM((n_chunk, others, block, chunk), bf16),
                pltpu.VMEM((n_chunk, block, chunk), f32),
                pltpu.VMEM((n_chunk, block, chunk), bf16),
                dma((kv_local, GROUP_WIDTH)),
                dma((kv_local, 2)),
                dma((n_chunk,)),
                dma((max(1, levels), kv_local)),
                dma((max(1, levels), kv_local)),
                dma((n_chunk,)),
                dma((n_chunk,)),
                dma((n_chunk, others)),
                dma((n_chunk, others)),
                dma((n_chunk,)),
            ],
            compiler_params=pltpu.CompilerParams(
                collective_id=0, has_side_effects=True, vmem_limit_bytes=48 * 1024 * 1024
            ),
            cost_estimate=pl.CostEstimate(
                flops=2 * rows * depth * width + 4 * rows * rows * (levels + 1) * depth,
                bytes_accessed=2 * depth * width,
                transcendentals=rows * rows * (levels + 1) * depth // HEAD_SIZE,
            ),
        )(queries, keys, values, out_weight)

    in_specs = (
        P(("grp", "seq"), "head"),
        P(("grp", "seq"), "head"),
        P(("grp", "seq"), "head"),
        P("head", None),
    )
    out_specs = P(("grp", "seq", "head"), None)
    return jax.shard_map(
        on_device, mesh=mesh, in_specs=in_specs, out_specs=out_specs, check_vma=False
    )
```

```python
import functools
import math

import jax
import jax.numpy as jnp
from jax import lax
from jax.experimental import pallas as pl
from jax.experimental.pallas import tpu as pltpu
from jax.sharding import PartitionSpec as P

QUERY_HEADS = 32
KEY_VALUE_HEADS = 16
HEAD_SIZE = 128
GROUP_WIDTH = QUERY_HEADS // KEY_VALUE_HEADS
CORES = 2
SUB_ROWS = (32, 48, 16)
MOST_COLUMNS = 1792

score_scale = 168.0 ** (-0.5) * math.log2(math.e)
MASKED = -1e30

MESH = pl.DeviceIdType.MESH


def layer_kernel(
    n_seq, n_head,
    q_hbm, k_hbm, v_hbm, w_hbm, out_hbm,
    q_buf, q_in, kv_buf, top, total, mix, attended, w_buf, partial, core_out, core_in,
    chip_out, chip_in, kept, out_buf, o_out, o_in, stat, stat_out, stat_in,
    q_sem, kv_sem, w_sem, z_send, z_recv, q_send, q_recv, o_send, o_recv, stat_send, stat_recv,
    core_send, core_recv, chip_send, chip_recv, out_sem,
):
    kv_local, _, rows, _ = kv_buf.shape[1:]
    n_col, _, chunk = w_buf.shape
    n_part, part_rows = attended.shape[:2]
    sub = part_rows // n_head
    n_step = n_part * n_col
    n_chip = n_head // CORES
    reaches = [1 << level for level in range(n_seq.bit_length() - 1)]
    hops = [1] + reaches[:-1] if reaches else []
    last = len(reaches) - 1
    seq = lax.axis_index("seq")
    head = lax.axis_index("head")
    chip, core = head // CORES, head % CORES
    core_peer = chip * CORES + 1 - core

    def columns(index, width):
        return pl.ds(pl.multiple_of(index * width, 128), width)

    def kv_load(c, which):
        source = (k_hbm, v_hbm)[which]
        return pltpu.make_async_copy(
            source.at[:, columns(c, HEAD_SIZE)], kv_buf.at[0, c, which], kv_sem.at[c, which]
        )

    def q_load(c, g, r):
        return pltpu.make_async_copy(
            q_hbm.at[:, r, :, columns(c * GROUP_WIDTH + g, HEAD_SIZE)],
            q_buf.at[c, g, r],
            q_sem.at[c, g, r],
        )

    def w_load(j):
        return pltpu.make_async_copy(w_hbm.at[:, columns(j, chunk)], w_buf.at[j], w_sem.at[j])

    def later(hop):
        return {"seq": lax.rem(seq + hop, n_seq)}

    def remote(source, target, send, recv, device):
        return pltpu.make_async_remote_copy(
            src_ref=source, dst_ref=target, send_sem=send, recv_sem=recv,
            device_id=device, device_id_type=MESH,
        )

    def z_copy(level, c):
        return remote(
            kv_buf.at[level, c], kv_buf.at[level + 1, c],
            z_send.at[level, c], z_recv.at[level, c], later(hops[level]),
        )

    def z_sends(level):
        needed = reaches[level - 1] if level else 0
        return jnp.logical_and(seq >= needed, seq + hops[level] < n_seq)

    def q_copy(c):
        return remote(
            q_buf.at[c], q_in.at[c], q_send.at[c], q_recv.at[c],
            {"seq": lax.rem(seq + n_seq - hops[last], n_seq)},
        )

    def o_copy(r):
        return remote(o_out.at[r], o_in.at[r], o_send.at[r], o_recv.at[r], later(hops[last]))

    def stat_copy(r):
        return remote(
            stat_out.at[r], stat_in.at[r], stat_send.at[r], stat_recv.at[r], later(hops[last])
        )

    if reaches:
        helped = seq >= reaches[last]
        helps = z_sends(last)

    def core_copy(i):
        return remote(
            core_out.at[i], core_in.at[i], core_send.at[i], core_recv.at[i], {"head": core_peer}
        )

    def chip_copy(i, offset):
        return remote(
            chip_out.at[i, offset - 1], chip_in.at[i, offset - 1],
            chip_send.at[i, offset - 1], chip_recv.at[i, offset - 1],
            {"head": lax.rem(chip + offset, n_chip) * CORES + core},
        )

    def out_copy(i):
        return pltpu.make_async_copy(
            out_buf.at[i], out_hbm.at[i // n_col, :, columns(i % n_col, chunk)], out_sem.at[i]
        )

    def loop(low, high, body):
        def step(i, carry):
            body(i)
            return carry

        lax.fori_loop(low, high, step, 0)

    barrier = pltpu.get_barrier_semaphore()
    expected = jnp.int32(n_chip)

    def greet(device):
        pl.semaphore_signal(barrier, inc=1, device_id=device, device_id_type=MESH)

    for distance in sorted(set(hops)):
        after, before = seq + distance < n_seq, seq >= distance

        @pl.when(after)
        def _():
            greet({"seq": seq + distance})

        @pl.when(before)
        def _():
            greet({"seq": seq - distance})

        expected += after.astype(jnp.int32) + before.astype(jnp.int32)
    greet({"head": core_peer})
    for offset in range(1, n_chip):
        greet({"head": lax.rem(chip + offset, n_chip) * CORES + core})

    def load_head(c):
        kv_load(c, 0).start()
        kv_load(c, 1).start()
        for g in range(GROUP_WIDTH):
            for r in range(n_part):
                q_load(c, g, r).start()

    loop(0, kv_local, load_head)
    pl.semaphore_wait(barrier, expected)

    def send_own(c):
        kv_load(c, 0).wait()
        kv_load(c, 1).wait()
        if last >= 1:
            @pl.when(z_sends(0))
            def _():
                z_copy(0, c).start()

        for g in range(GROUP_WIDTH):
            for r in range(n_part):
                q_load(c, g, r).wait()
        if reaches:
            @pl.when(helped)
            def _():
                q_copy(c).start()

    loop(0, kv_local, send_own)
    loop(0, n_col, lambda j: w_load(j).start())
    stat[...] = jnp.zeros_like(stat)

    stacked = GROUP_WIDTH * rows
    by_part = (GROUP_WIDTH, n_part, part_rows)

    def scores_of(q_ref, level, c):
        return score_scale * lax.dot_general(
            q_ref[c].reshape(stacked, HEAD_SIZE), kv_buf[level, c, 0], (((1,), (1,)), ((), ())),
            preferred_element_type=jnp.float32,
        )

    def mixed_values(level, c, shifted):
        return jnp.dot(
            shifted.astype(jnp.bfloat16), kv_buf[level, c, 1], preferred_element_type=jnp.float32
        ).reshape(by_part + (HEAD_SIZE,))

    def own_block(c):
        shape = (GROUP_WIDTH, n_part, n_head, sub, rows)
        token = (
            lax.broadcasted_iota(jnp.int32, shape, 1) * sub
            + lax.broadcasted_iota(jnp.int32, shape, 2) * (sub * n_part)
            + lax.broadcasted_iota(jnp.int32, shape, 3)
        )
        causal = token >= lax.broadcasted_iota(jnp.int32, shape, 4)
        scores = scores_of(q_buf, 0, c).reshape(shape)
        scores = jnp.where(causal, scores, MASKED).reshape(stacked, rows)
        row_max = jnp.max(scores, axis=-1, keepdims=True)
        shifted = jnp.exp2(scores - row_max)
        top[c] = row_max.reshape(by_part + (1,))
        total[c] = jnp.sum(shifted, axis=-1, keepdims=True).reshape(by_part + (1,))
        mix[c] = mixed_values(0, c, shifted)

    def earlier_block(level, c):
        scores = scores_of(q_buf, level, c)
        before = top[c].reshape(stacked, 1)
        row_max = jnp.maximum(before, jnp.max(scores, axis=-1, keepdims=True))
        fade = jnp.exp2(before - row_max)
        shifted = jnp.exp2(scores - row_max)
        fade = fade.reshape(by_part + (1,))
        top[c] = row_max.reshape(by_part + (1,))
        total[c] = total[c] * fade + jnp.sum(shifted, axis=-1, keepdims=True).reshape(
            by_part + (1,)
        )
        mix[c] = mix[c] * fade + mixed_values(level, c, shifted)

    def help_later(c):
        q_copy(c).wait_recv()
        scores = scores_of(q_in, last, c)
        row_max = jnp.max(scores, axis=-1, keepdims=True)
        shifted = jnp.exp2(scores - row_max)
        row_sum = jnp.sum(shifted, axis=-1, keepdims=True)
        log_sum = (row_max + jnp.log2(row_sum)).reshape(by_part + (1,))
        result = mixed_values(last, c, shifted) / row_sum.reshape(by_part + (1,))
        lane = lax.broadcasted_iota(jnp.int32, stat.shape[1:], 1)
        for g in range(GROUP_WIDTH):
            for r in range(n_part):
                o_out[r, c, g] = result[g, r].astype(jnp.bfloat16)
                stat[r] = jnp.where(lane == c * GROUP_WIDTH + g, log_sum[g, r], stat[r])

    loop(0, kv_local, own_block)
    for level in range(1, last + 1):

        @pl.when(seq >= reaches[level - 1])
        def _():
            def arrived(c):
                z_copy(level - 1, c).wait_recv()
                if level < last:
                    @pl.when(z_sends(level))
                    def _():
                        z_copy(level, c).start()
                else:
                    @pl.when(helps)
                    def _():
                        help_later(c)

                earlier_block(level, c)

            loop(0, kv_local, arrived)

    if reaches:

        @pl.when(helps)
        def _():
            if last == 0:
                loop(0, kv_local, help_later)

            def hand_over(r):
                stat_out[r] = stat[r].T[: stat_out.shape[1]]
                stat_copy(r).start()
                o_copy(r).start()

            loop(0, n_part, hand_over)

    def finish_alone(r):
        for c in range(kv_local):
            for g in range(GROUP_WIDTH):
                h = c * GROUP_WIDTH + g
                attended[r, :, h * HEAD_SIZE : (h + 1) * HEAD_SIZE] = (
                    mix[c, g, r] / total[c, g, r]
                ).astype(jnp.bfloat16)

    def finish_helped(r):
        stat_copy(r).wait_recv()
        o_copy(r).wait_recv()
        log_sums = stat_in[r].T
        for c in range(kv_local):
            for g in range(GROUP_WIDTH):
                h = c * GROUP_WIDTH + g
                log_sum = log_sums[:, h : h + 1]
                row_max = jnp.maximum(top[c, g, r], log_sum)
                here, there = jnp.exp2(top[c, g, r] - row_max), jnp.exp2(log_sum - row_max)
                summed = mix[c, g, r] * here + o_in[r, c, g].astype(jnp.float32) * there
                attended[r, :, h * HEAD_SIZE : (h + 1) * HEAD_SIZE] = (
                    summed / (total[c, g, r] * here + there)
                ).astype(jnp.bfloat16)

    def project(r, j):
        i = r * n_col + j
        slot = lax.rem(i, 2)

        @pl.when(r == 0)
        def _():
            w_load(j).wait()

        partial[slot] = jnp.dot(attended[r], w_buf[j], preferred_element_type=jnp.float32)
        for x in range(n_chip):
            start = pl.multiple_of((x * CORES + 1 - core) * sub, 8)
            core_out[i, x] = partial[slot, pl.ds(start, sub), :].astype(jnp.bfloat16)
        core_copy(i).start()

    def exchange(i):
        slot = lax.rem(i, 2)
        core_copy(i).wait_recv()

        def both_cores(x):
            start = pl.multiple_of((x * CORES + core) * sub, 8)
            return partial[slot, pl.ds(start, sub), :] + core_in[i, x].astype(jnp.float32)

        for offset in range(1, n_chip):
            chip_out[i, offset - 1] = both_cores(lax.rem(chip + offset, n_chip)).astype(
                jnp.bfloat16
            )
            chip_copy(i, offset).start()
        kept[i] = both_cores(chip)

    def collect(i):
        summed = kept[i]
        for offset in range(1, n_chip):
            chip_copy(i, offset).wait_recv()
            summed += chip_in[i, offset - 1].astype(jnp.float32)
        out_buf[i] = summed.astype(jnp.bfloat16)
        out_copy(i).start()

    def row_part(r):
        if reaches:
            @pl.when(helped)
            def _():
                finish_helped(r)

            @pl.when(jnp.logical_not(helped))
            def _():
                finish_alone(r)
        else:
            finish_alone(r)
        project(r, 0)

        def step(j):
            project(r, j)
            exchange(r * n_col + j - 1)

        loop(1, n_col, step)
        exchange(r * n_col + n_col - 1)

    loop(0, n_part, row_part)
    loop(0, n_step, collect)

    def settle(i):
        core_copy(i).wait_send()
        for offset in range(1, n_chip):
            chip_copy(i, offset).wait_send()
        out_copy(i).wait()

    loop(0, n_step, settle)
    for level in range(last):

        @pl.when(z_sends(level))
        def _():
            loop(0, kv_local, lambda c: z_copy(level, c).wait_send())

    if reaches:

        @pl.when(helped)
        def _():
            loop(0, kv_local, lambda c: q_copy(c).wait_send())

        @pl.when(helps)
        def _():
            def sent(r):
                stat_copy(r).wait_send()
                o_copy(r).wait_send()

            loop(0, n_part, sent)


def solution(mesh):
    n_seq, n_head = mesh.shape["seq"], mesh.shape["head"]

    def on_device(queries, keys, values, out_weight):
        rows = queries.shape[0]
        depth, width = out_weight.shape
        kv_local = keys.shape[1] // HEAD_SIZE
        heads = kv_local * GROUP_WIDTH
        block = rows // n_head
        n_chip = n_head // CORES
        levels = max(1, n_seq.bit_length() - 1)
        sub = next((s for s in SUB_ROWS if block % s == 0), block)
        n_part = block // sub
        part_rows = n_head * sub
        chunk = max(c for c in range(128, MOST_COLUMNS + 1, 128) if width % c == 0)
        n_col = width // chunk
        n_step = n_part * n_col
        bf16, f32, dma = jnp.bfloat16, jnp.float32, pltpu.SemaphoreType.DMA
        anywhere = pl.BlockSpec(memory_space=pl.ANY)
        others = max(1, n_chip - 1)
        stat_rows = -(-heads // 8) * 8
        by_part = (kv_local, GROUP_WIDTH, n_part, part_rows)
        result = pl.pallas_call(
            functools.partial(layer_kernel, n_seq, n_head),
            out_shape=jax.ShapeDtypeStruct((n_part, sub, width), bf16),
            in_specs=[anywhere] * 4,
            out_specs=anywhere,
            scratch_shapes=[
                pltpu.VMEM((kv_local, GROUP_WIDTH, n_part, n_head, sub, HEAD_SIZE), bf16),
                pltpu.VMEM((kv_local, GROUP_WIDTH, n_part, n_head, sub, HEAD_SIZE), bf16),
                pltpu.VMEM((levels, kv_local, 2, rows, HEAD_SIZE), bf16),
                pltpu.VMEM(by_part + (1,), f32),
                pltpu.VMEM(by_part + (1,), f32),
                pltpu.VMEM(by_part + (HEAD_SIZE,), f32),
                pltpu.VMEM((n_part, part_rows, depth), bf16),
                pltpu.VMEM((n_col, depth, chunk), bf16),
                pltpu.VMEM((2, part_rows, chunk), f32),
                pltpu.VMEM((n_step, n_chip, sub, chunk), bf16),
                pltpu.VMEM((n_step, n_chip, sub, chunk), bf16),
                pltpu.VMEM((n_step, others, sub, chunk), bf16),
                pltpu.VMEM((n_step, others, sub, chunk), bf16),
                pltpu.VMEM((n_step, sub, chunk), f32),
                pltpu.VMEM((n_step, sub, chunk), bf16),
                pltpu.VMEM((n_part, kv_local, GROUP_WIDTH, part_rows, HEAD_SIZE), bf16),
                pltpu.VMEM((n_part, kv_local, GROUP_WIDTH, part_rows, HEAD_SIZE), bf16),
                pltpu.VMEM((n_part, part_rows, 128), f32),
                pltpu.VMEM((n_part, stat_rows, part_rows), f32),
                pltpu.VMEM((n_part, stat_rows, part_rows), f32),
                dma((kv_local, GROUP_WIDTH, n_part)),
                dma((kv_local, 2)),
                dma((n_col,)),
                dma((levels, kv_local)),
                dma((levels, kv_local)),
                dma((kv_local,)),
                dma((kv_local,)),
                dma((n_part,)),
                dma((n_part,)),
                dma((n_part,)),
                dma((n_part,)),
                dma((n_step,)),
                dma((n_step,)),
                dma((n_step, others)),
                dma((n_step, others)),
                dma((n_step,)),
            ],
            compiler_params=pltpu.CompilerParams(
                collective_id=0, has_side_effects=True, vmem_limit_bytes=60 * 1024 * 1024
            ),
            cost_estimate=pl.CostEstimate(
                flops=2 * rows * depth * width + 4 * rows * rows * (levels + 1) * depth,
                bytes_accessed=2 * depth * width,
                transcendentals=rows * rows * (levels + 1) * depth // HEAD_SIZE,
            ),
        )(queries.reshape(n_head, n_part, sub, -1), keys, values, out_weight)
        return result.reshape(block, width)

    in_specs = (
        P(("grp", "seq"), "head"),
        P(("grp", "seq"), "head"),
        P(("grp", "seq"), "head"),
        P("head", None),
    )
    out_specs = P(("grp", "seq", "head"), None)
    return jax.shard_map(
        on_device, mesh=mesh, in_specs=in_specs, out_specs=out_specs, check_vma=False
    )
```

```python
import functools
import math

import jax
import jax.numpy as jnp
from jax import lax
from jax.experimental import pallas as pl
from jax.experimental.pallas import tpu as pltpu
from jax.sharding import PartitionSpec as P

QUERY_HEADS = 32
KEY_VALUE_HEADS = 16
HEAD_SIZE = 128
GROUP_WIDTH = QUERY_HEADS // KEY_VALUE_HEADS
CORES = 2
SUB_ROWS = (32, 48, 16)
MOST_COLUMNS = 1792

score_scale = 168.0 ** (-0.5) * math.log2(math.e)
MASKED = -1e30

MESH = pl.DeviceIdType.MESH


def layer_kernel(
    n_seq, n_head,
    q_hbm, k_hbm, v_hbm, w_hbm, out_hbm,
    q_buf, q_in, kv_buf, top, total, mix, attended, w_buf, partial, core_out, core_in,
    chip_out, chip_in, kept, out_buf, o_out, o_in, stat, stat_out, stat_in,
    q_sem, kv_sem, w_sem, z_send, z_recv, q_send, q_recv, o_send, o_recv, stat_send, stat_recv,
    core_send, core_recv, chip_send, chip_recv, out_sem,
):
    kv_local, _, rows, _ = kv_buf.shape[1:]
    n_col, _, chunk = w_buf.shape
    n_part, part_rows = attended.shape[:2]
    sub = part_rows // n_head
    n_step = n_part * n_col
    n_chip = n_head // CORES
    reaches = [1 << level for level in range(n_seq.bit_length() - 1)]
    hops = [1] + reaches[:-1] if reaches else []
    last = len(reaches) - 1
    seq = lax.axis_index("seq")
    head = lax.axis_index("head")
    chip, core = head // CORES, head % CORES
    core_peer = chip * CORES + 1 - core

    def columns(index, width):
        return pl.ds(pl.multiple_of(index * width, 128), width)

    def kv_load(c, which):
        source = (k_hbm, v_hbm)[which]
        return pltpu.make_async_copy(
            source.at[:, columns(c, HEAD_SIZE)], kv_buf.at[0, c, which], kv_sem.at[c, which]
        )

    def q_load(c, g, r):
        return pltpu.make_async_copy(
            q_hbm.at[:, r, :, columns(c * GROUP_WIDTH + g, HEAD_SIZE)],
            q_buf.at[c, g, r],
            q_sem.at[c, g, r],
        )

    def w_load(j):
        return pltpu.make_async_copy(w_hbm.at[:, columns(j, chunk)], w_buf.at[j], w_sem.at[j])

    def later(hop):
        return {"seq": lax.rem(seq + hop, n_seq)}

    def remote(source, target, send, recv, device):
        return pltpu.make_async_remote_copy(
            src_ref=source, dst_ref=target, send_sem=send, recv_sem=recv,
            device_id=device, device_id_type=MESH,
        )

    def z_copy(level, c):
        return remote(
            kv_buf.at[level, c], kv_buf.at[level + 1, c],
            z_send.at[level, c], z_recv.at[level, c], later(hops[level]),
        )

    def z_sends(level):
        needed = reaches[level - 1] if level else 0
        return jnp.logical_and(seq >= needed, seq + hops[level] < n_seq)

    def q_copy(c):
        return remote(
            q_buf.at[c], q_in.at[c], q_send.at[c], q_recv.at[c],
            {"seq": lax.rem(seq + n_seq - hops[last], n_seq)},
        )

    def o_copy(r):
        return remote(o_out.at[r], o_in.at[r], o_send.at[r], o_recv.at[r], later(hops[last]))

    def stat_copy(r):
        return remote(
            stat_out.at[r], stat_in.at[r], stat_send.at[r], stat_recv.at[r], later(hops[last])
        )

    if reaches:
        helped = seq >= reaches[last]
        helps = z_sends(last)

    def core_copy(i):
        return remote(
            core_out.at[i], core_in.at[i], core_send.at[i], core_recv.at[i], {"head": core_peer}
        )

    def chip_copy(i, offset):
        return remote(
            chip_out.at[i, offset - 1], chip_in.at[i, offset - 1],
            chip_send.at[i, offset - 1], chip_recv.at[i, offset - 1],
            {"head": lax.rem(chip + offset, n_chip) * CORES + core},
        )

    def out_copy(i):
        return pltpu.make_async_copy(
            out_buf.at[i], out_hbm.at[i // n_col, :, columns(i % n_col, chunk)], out_sem.at[i]
        )

    def loop(low, high, body):
        def step(i, carry):
            body(i)
            return carry

        lax.fori_loop(low, high, step, 0)

    barrier = pltpu.get_barrier_semaphore()
    expected = jnp.int32(n_chip)

    def greet(device):
        pl.semaphore_signal(barrier, inc=1, device_id=device, device_id_type=MESH)

    for distance in sorted(set(hops)):
        after, before = seq + distance < n_seq, seq >= distance

        @pl.when(after)
        def _():
            greet({"seq": seq + distance})

        @pl.when(before)
        def _():
            greet({"seq": seq - distance})

        expected += after.astype(jnp.int32) + before.astype(jnp.int32)
    greet({"head": core_peer})
    for offset in range(1, n_chip):
        greet({"head": lax.rem(chip + offset, n_chip) * CORES + core})

    def load_head(c):
        kv_load(c, 0).start()
        kv_load(c, 1).start()
        for g in range(GROUP_WIDTH):
            for r in range(n_part):
                q_load(c, g, r).start()

    loop(0, kv_local, load_head)
    pl.semaphore_wait(barrier, expected)

    def loaded(c):
        kv_load(c, 0).wait()
        kv_load(c, 1).wait()
        for g in range(GROUP_WIDTH):
            for r in range(n_part):
                q_load(c, g, r).wait()

    def start_own(c):
        if last >= 1:
            @pl.when(z_sends(0))
            def _():
                z_copy(0, c).start()

        if reaches:
            @pl.when(helped)
            def _():
                q_copy(c).start()

    def sent_own(c):
        if last >= 1:
            @pl.when(z_sends(0))
            def _():
                z_copy(0, c).wait_send()

        if reaches:
            @pl.when(helped)
            def _():
                q_copy(c).wait_send()

    loaded(0)
    start_own(0)
    loop(1, kv_local, loaded)
    loop(0, n_col, lambda j: w_load(j).start())
    stat[...] = jnp.zeros_like(stat)

    stacked = GROUP_WIDTH * rows
    by_part = (GROUP_WIDTH, n_part, part_rows)

    def scores_of(q_ref, level, c):
        return score_scale * lax.dot_general(
            q_ref[c].reshape(stacked, HEAD_SIZE), kv_buf[level, c, 0], (((1,), (1,)), ((), ())),
            preferred_element_type=jnp.float32,
        )

    def mixed_values(level, c, shifted):
        return jnp.dot(
            shifted.astype(jnp.bfloat16), kv_buf[level, c, 1], preferred_element_type=jnp.float32
        ).reshape(by_part + (HEAD_SIZE,))

    def own_block(c):
        shape = (GROUP_WIDTH, n_part, n_head, sub, rows)
        token = (
            lax.broadcasted_iota(jnp.int32, shape, 1) * sub
            + lax.broadcasted_iota(jnp.int32, shape, 2) * (sub * n_part)
            + lax.broadcasted_iota(jnp.int32, shape, 3)
        )
        causal = token >= lax.broadcasted_iota(jnp.int32, shape, 4)
        scores = scores_of(q_buf, 0, c).reshape(shape)
        scores = jnp.where(causal, scores, MASKED).reshape(stacked, rows)
        row_max = jnp.max(scores, axis=-1, keepdims=True)
        shifted = jnp.exp2(scores - row_max)
        top[c] = row_max.reshape(by_part + (1,))
        total[c] = jnp.sum(shifted, axis=-1, keepdims=True).reshape(by_part + (1,))
        mix[c] = mixed_values(0, c, shifted)

    def earlier_block(level, c):
        scores = scores_of(q_buf, level, c)
        before = top[c].reshape(stacked, 1)
        row_max = jnp.maximum(before, jnp.max(scores, axis=-1, keepdims=True))
        fade = jnp.exp2(before - row_max)
        shifted = jnp.exp2(scores - row_max)
        fade = fade.reshape(by_part + (1,))
        top[c] = row_max.reshape(by_part + (1,))
        total[c] = total[c] * fade + jnp.sum(shifted, axis=-1, keepdims=True).reshape(
            by_part + (1,)
        )
        mix[c] = mix[c] * fade + mixed_values(level, c, shifted)

    def help_later(c):
        q_copy(c).wait_recv()
        scores = scores_of(q_in, last, c)
        row_max = jnp.max(scores, axis=-1, keepdims=True)
        shifted = jnp.exp2(scores - row_max)
        row_sum = jnp.sum(shifted, axis=-1, keepdims=True)
        log_sum = (row_max + jnp.log2(row_sum)).reshape(by_part + (1,))
        result = mixed_values(last, c, shifted) / row_sum.reshape(by_part + (1,))
        lane = lax.broadcasted_iota(jnp.int32, stat.shape[1:], 1)
        for g in range(GROUP_WIDTH):
            for r in range(n_part):
                o_out[r, c, g] = result[g, r].astype(jnp.bfloat16)
                stat[r] = jnp.where(lane == c * GROUP_WIDTH + g, log_sum[g, r], stat[r])

    def hand_over(r):
        stat_out[r] = stat[r].T[: stat_out.shape[1]]
        stat_copy(r).start()
        o_copy(r).start()

    def hand_next(r):
        if reaches:
            @pl.when(helps)
            def _():
                stat_copy(r).wait_send()
                o_copy(r).wait_send()

                @pl.when(r + 1 < n_part)
                def _():
                    hand_over(r + 1)

    def arrived(level, c):
        @pl.when(seq >= reaches[level - 1])
        def _():
            z_copy(level - 1, c).wait_recv()
            if level < last:
                @pl.when(z_sends(level))
                def _():
                    z_copy(level, c).start()
            else:
                @pl.when(helps)
                def _():
                    help_later(c)

                    @pl.when(c == kv_local - 1)
                    def _():
                        hand_over(0)

            earlier_block(level, c)

    def first_pass(c):
        @pl.when(c + 1 < kv_local)
        def _():
            own_block(c + 1)

        sent_own(c)

        @pl.when(c + 1 < kv_local)
        def _():
            start_own(c + 1)

        if last >= 1:
            arrived(1, c)

    own_block(0)
    loop(0, kv_local, first_pass)
    for level in range(2, last + 1):
        loop(0, kv_local, functools.partial(arrived, level))
    if last == 0:

        @pl.when(helps)
        def _():
            loop(0, kv_local, help_later)
            hand_over(0)

    def finish_alone(r):
        for c in range(kv_local):
            for g in range(GROUP_WIDTH):
                h = c * GROUP_WIDTH + g
                attended[r, :, h * HEAD_SIZE : (h + 1) * HEAD_SIZE] = (
                    mix[c, g, r] / total[c, g, r]
                ).astype(jnp.bfloat16)

    def finish_helped(r):
        stat_copy(r).wait_recv()
        o_copy(r).wait_recv()
        log_sums = stat_in[r].T
        for c in range(kv_local):
            for g in range(GROUP_WIDTH):
                h = c * GROUP_WIDTH + g
                log_sum = log_sums[:, h : h + 1]
                row_max = jnp.maximum(top[c, g, r], log_sum)
                here, there = jnp.exp2(top[c, g, r] - row_max), jnp.exp2(log_sum - row_max)
                summed = mix[c, g, r] * here + o_in[r, c, g].astype(jnp.float32) * there
                attended[r, :, h * HEAD_SIZE : (h + 1) * HEAD_SIZE] = (
                    summed / (total[c, g, r] * here + there)
                ).astype(jnp.bfloat16)

    def project(r, j):
        i = r * n_col + j
        slot = lax.rem(i, 2)

        @pl.when(r == 0)
        def _():
            w_load(j).wait()

        partial[slot] = jnp.dot(attended[r], w_buf[j], preferred_element_type=jnp.float32)
        for x in range(n_chip):
            start = pl.multiple_of((x * CORES + 1 - core) * sub, 8)
            core_out[i, x] = partial[slot, pl.ds(start, sub), :].astype(jnp.bfloat16)
        core_copy(i).start()

    def exchange(i):
        slot = lax.rem(i, 2)
        core_copy(i).wait_recv()

        def both_cores(x):
            start = pl.multiple_of((x * CORES + core) * sub, 8)
            return partial[slot, pl.ds(start, sub), :] + core_in[i, x].astype(jnp.float32)

        for offset in range(1, n_chip):
            chip_out[i, offset - 1] = both_cores(lax.rem(chip + offset, n_chip)).astype(
                jnp.bfloat16
            )
            chip_copy(i, offset).start()
        kept[i] = both_cores(chip)

    def collect(i):
        summed = kept[i]
        for offset in range(1, n_chip):
            chip_copy(i, offset).wait_recv()
            summed += chip_in[i, offset - 1].astype(jnp.float32)
        out_buf[i] = summed.astype(jnp.bfloat16)
        out_copy(i).start()

    def row_part(r):
        if reaches:
            @pl.when(helped)
            def _():
                hand_next(r)
                finish_helped(r)

            @pl.when(jnp.logical_not(helped))
            def _():
                finish_alone(r)
        else:
            finish_alone(r)
        project(r, 0)

        def step(j):
            project(r, j)
            exchange(r * n_col + j - 1)

        loop(1, n_col, step)
        exchange(r * n_col + n_col - 1)
        if reaches:

            @pl.when(jnp.logical_not(helped))
            def _():
                hand_next(r)

    loop(0, n_part, row_part)
    loop(0, n_step, collect)

    def settle(i):
        core_copy(i).wait_send()
        for offset in range(1, n_chip):
            chip_copy(i, offset).wait_send()
        out_copy(i).wait()

    loop(0, n_step, settle)
    for level in range(1, last):

        @pl.when(z_sends(level))
        def _():
            loop(0, kv_local, lambda c: z_copy(level, c).wait_send())


def solution(mesh):
    n_seq, n_head = mesh.shape["seq"], mesh.shape["head"]

    def on_device(queries, keys, values, out_weight):
        rows = queries.shape[0]
        depth, width = out_weight.shape
        kv_local = keys.shape[1] // HEAD_SIZE
        heads = kv_local * GROUP_WIDTH
        block = rows // n_head
        n_chip = n_head // CORES
        levels = max(1, n_seq.bit_length() - 1)
        sub = next((s for s in SUB_ROWS if block % s == 0), block)
        n_part = block // sub
        part_rows = n_head * sub
        chunk = max(c for c in range(128, MOST_COLUMNS + 1, 128) if width % c == 0)
        n_col = width // chunk
        n_step = n_part * n_col
        bf16, f32, dma = jnp.bfloat16, jnp.float32, pltpu.SemaphoreType.DMA
        anywhere = pl.BlockSpec(memory_space=pl.ANY)
        others = max(1, n_chip - 1)
        stat_rows = -(-heads // 8) * 8
        by_part = (kv_local, GROUP_WIDTH, n_part, part_rows)
        result = pl.pallas_call(
            functools.partial(layer_kernel, n_seq, n_head),
            out_shape=jax.ShapeDtypeStruct((n_part, sub, width), bf16),
            in_specs=[anywhere] * 4,
            out_specs=anywhere,
            scratch_shapes=[
                pltpu.VMEM((kv_local, GROUP_WIDTH, n_part, n_head, sub, HEAD_SIZE), bf16),
                pltpu.VMEM((kv_local, GROUP_WIDTH, n_part, n_head, sub, HEAD_SIZE), bf16),
                pltpu.VMEM((levels, kv_local, 2, rows, HEAD_SIZE), bf16),
                pltpu.VMEM(by_part + (1,), f32),
                pltpu.VMEM(by_part + (1,), f32),
                pltpu.VMEM(by_part + (HEAD_SIZE,), f32),
                pltpu.VMEM((n_part, part_rows, depth), bf16),
                pltpu.VMEM((n_col, depth, chunk), bf16),
                pltpu.VMEM((2, part_rows, chunk), f32),
                pltpu.VMEM((n_step, n_chip, sub, chunk), bf16),
                pltpu.VMEM((n_step, n_chip, sub, chunk), bf16),
                pltpu.VMEM((n_step, others, sub, chunk), bf16),
                pltpu.VMEM((n_step, others, sub, chunk), bf16),
                pltpu.VMEM((n_step, sub, chunk), f32),
                pltpu.VMEM((n_step, sub, chunk), bf16),
                pltpu.VMEM((n_part, kv_local, GROUP_WIDTH, part_rows, HEAD_SIZE), bf16),
                pltpu.VMEM((n_part, kv_local, GROUP_WIDTH, part_rows, HEAD_SIZE), bf16),
                pltpu.VMEM((n_part, part_rows, 128), f32),
                pltpu.VMEM((n_part, stat_rows, part_rows), f32),
                pltpu.VMEM((n_part, stat_rows, part_rows), f32),
                dma((kv_local, GROUP_WIDTH, n_part)),
                dma((kv_local, 2)),
                dma((n_col,)),
                dma((levels, kv_local)),
                dma((levels, kv_local)),
                dma((kv_local,)),
                dma((kv_local,)),
                dma((n_part,)),
                dma((n_part,)),
                dma((n_part,)),
                dma((n_part,)),
                dma((n_step,)),
                dma((n_step,)),
                dma((n_step, others)),
                dma((n_step, others)),
                dma((n_step,)),
            ],
            compiler_params=pltpu.CompilerParams(
                collective_id=0, has_side_effects=True, vmem_limit_bytes=60 * 1024 * 1024
            ),
            cost_estimate=pl.CostEstimate(
                flops=2 * rows * depth * width + 4 * rows * rows * (levels + 1) * depth,
                bytes_accessed=2 * depth * width,
                transcendentals=rows * rows * (levels + 1) * depth // HEAD_SIZE,
            ),
        )(queries.reshape(n_head, n_part, sub, -1), keys, values, out_weight)
        return result.reshape(block, width)

    in_specs = (
        P(("grp", "seq"), "head"),
        P(("grp", "seq"), "head"),
        P(("grp", "seq"), "head"),
        P("head", None),
    )
    out_specs = P(("grp", "seq", "head"), None)
    return jax.shard_map(
        on_device, mesh=mesh, in_specs=in_specs, out_specs=out_specs, check_vma=False
    )
```
